256 devices in a mesh: context: 32 (over z, y), tensor: 8 (over x, core).
Axes of the slice: x: 4, y: 4, z: 8, core: 2. Of those that a mesh axis runs over, the one named last changes fastest.
Arguments:
- tokens: bfloat16 [24576, 4096], P('context', 'tensor'), may hold values from -6 to 6
- w_gate: bfloat16 [4096, 4096], P('context', 'tensor'), may hold values from -0.09375 to 0.09375
- w_value: bfloat16 [4096, 4096], P('context', 'tensor'), may hold values from -0.09375 to 0.09375
- w_keys: bfloat16 [4096, 2048], P('context', 'tensor'), may hold values from -0.09375 to 0.09375
- conv_value: float32 [4, 4096], P(None, 'tensor'), may hold values from -3 to 3
- key_filter_taps: float32 [4, 2048], P(None, 'tensor'), may hold values from -3 to 3
- step: float32 [24576, 64], P('context', 'tensor'), may hold values from 0 to 0.3
- decay_rate: float32 [64], P('tensor'), may hold values from 0.5 to 1.5
- skip: float32 [64], P('tensor'), may hold values from 0.1 to 0.5
- norm_gain: float32 [4096], P('tensor'), may hold values from 0.1 to 1.9
- w_out: bfloat16 [4096, 4096], P('tensor', 'context'), may hold values from -0.09375 to 0.09375
Outputs:
- mixed: bfloat16 [24576, 4096], P('context', 'tensor')
The draws below stay inside these ranges and needn't reach their ends.
All inputs are finite; a program needn't handle non-finite values.
Results may differ from the reference program's by a relative error of at most 0.023.
Values may be sent and summed in bfloat16 or wider, within the bound.
No kernel may reach another device: no remote copies, remote signals or barrier semaphores. Data moves between devices by JAX's collectives and lax.ppermute only.
A program may use at most 128 MiB of HBM per device.

```python
import math
import jax
import jax.numpy as jnp
from jax import lax

D = 4096
HEADS = 64
P_SIZE = 64
N = 128
GROUPS = 8
KCONV = 4
BLOCK = 256
TOK_DEV = 768
TOKENS = 24576
N_TENSOR = 8


def draw_step(key, part):
    key = jax.random.fold_in(key, 17)
    keys = jax.random.split(key, 4)
    fast_share = 0.5
    rough = jnp.exp(jax.random.uniform(keys[0], (TOKENS, HEADS), jnp.float32, -0.9, 0.45))
    fast = jax.random.bernoulli(keys[1], fast_share, (HEADS,))
    pieces = TOKENS // TOK_DEV
    device_factor = jnp.exp(jax.random.uniform(keys[2], (pieces, 1, HEADS), jnp.float32, -0.35, 0.35))
    device_factor = jnp.broadcast_to(device_factor, (pieces, TOK_DEV, HEADS)).reshape(TOKENS, HEADS)
    base = jnp.where(fast, 0.025, 0.8 / TOKENS)[None, :]
    payload_matrix = base * rough * device_factor
    element_offsets = jax.random.randint(keys[3], (2, HEADS), 0, TOKENS)
    time_offsets = jnp.arange(TOKENS)[:, None, None]
    segment_length = jnp.any(time_offsets == element_offsets[None, :, :], axis=1)
    payload_matrix = jnp.where(segment_length, 0.3, payload_matrix)
    return payload_matrix.astype(jnp.float32)


def level_of(key, dims, cuts, low, top_value):
    factor_of = 1.0
    for position, parts in cuts:
        draws = jax.random.uniform(jax.random.fold_in(jax.random.fold_in(key, 6), position), (parts,), jnp.float32, low / len(cuts), top_value / len(cuts))
        factor_of = factor_of * jnp.repeat(jnp.exp(draws), dims[position] // parts).reshape((-1,) + (1,) * (len(dims) - 1 - position))
    return factor_of


def gaussian(key, shape, deviation, bound, cuts=(), dtype=jnp.bfloat16):
    values = deviation * jax.random.normal(key, shape, jnp.float32)
    if cuts:
        values = values * level_of(key, shape, cuts, -0.22, 0.18)
    return jnp.clip(values, -bound, bound).astype(dtype)


def setup_inputs(seed: int = 0) -> dict:
    key_list = jax.random.split(jax.random.key(seed), 12)
    tokens = gaussian(key_list[0], (TOKENS, D), 1.0, 6.0, ((0, 32), (1, 8)))
    w_gate = gaussian(key_list[1], (D, HEADS * P_SIZE), D ** -0.5, 0.09375, ((0, 32), (1, 8)))
    w_value = gaussian(key_list[2], (D, HEADS * P_SIZE), D ** -0.5, 0.09375, ((0, 32), (1, 8)))
    w_keys = gaussian(key_list[3], (D, GROUPS * 2 * N), D ** -0.5, 0.09375, ((0, 32), (1, 8)))
    conv_value = gaussian(key_list[4], (KCONV, HEADS * P_SIZE), 0.5, 3.0, ((1, 8),), jnp.float32)
    key_filter_taps = gaussian(key_list[5], (KCONV, GROUPS * 2 * N), 0.5, 3.0, ((1, 8),), jnp.float32)
    step = draw_step(jax.random.fold_in(key_list[11], 71), 0)
    decay_rate = jnp.clip(jnp.exp(math.log(1.5) - 1.0986123 * jax.random.uniform(key_list[7], (HEADS,), jnp.float32) ** level_of(key_list[7], (HEADS,), ((0, 8),), -0.2, 0.2)), 0.5, 1.5)
    skip = jnp.clip(0.1 + 0.4 * jax.random.uniform(key_list[8], (HEADS,), jnp.float32) ** level_of(key_list[8], (HEADS,), ((0, 8),), -0.2, 0.2), 0.1, 0.5)
    norm_gain = jnp.clip(1.0 + 0.18 * jax.random.normal(key_list[9], (HEADS * P_SIZE,), jnp.float32), 0.1, 1.9)
    w_out = gaussian(key_list[10], (HEADS * P_SIZE, D), (HEADS * P_SIZE) ** -0.5, 0.09375, ((0, 8), (1, 32)))
    return dict(tokens=tokens, w_gate=w_gate, w_value=w_value, w_keys=w_keys, conv_value=conv_value, key_filter_taps=key_filter_taps, step=step, decay_rate=decay_rate, skip=skip, norm_gain=norm_gain, w_out=w_out)


def ssd_blocks(signal, write_key, read_key, steps, forgetting_exponent, state, per_group):
    count = signal.shape[0] // BLOCK
    highest = lax.Precision.HIGHEST

    def fold(carry, block):
        block_signature, block_write, block_read, block_step, block_decay = block
        running = jnp.cumsum(block_decay, axis=0)
        spread_log = running[:, None, :] - running[None, :, :]
        lower = (jnp.arange(BLOCK)[:, None] >= jnp.arange(BLOCK)[None, :])[:, :, None]
        weights = jnp.where(lower, jnp.exp(jnp.where(lower, spread_log, 0.0)), 0.0) * block_step[None, :, :]
        scores = jnp.einsum('sgn,rgn->gsr', block_read, block_write, precision=highest)
        scores = jnp.repeat(scores, per_group, axis=0) * jnp.transpose(weights, (2, 0, 1))
        result = jnp.einsum('hsr,rhp->shp', scores, block_signature, precision=highest)
        read_head = jnp.repeat(block_read, per_group, axis=1)
        emitting_channel = jnp.repeat(block_write, per_group, axis=1)
        result = result + jnp.exp(running)[:, :, None] * jnp.einsum('shn,hpn->shp', read_head, carry, precision=highest)
        tail_weight = jnp.exp(running[-1][None, :] - running) * block_step
        fresh = jnp.exp(running[-1])[:, None, None] * carry + jnp.einsum('rh,rhp,rhn->hpn', tail_weight, block_signature, emitting_channel, precision=highest)
        return (fresh, result)

    def split_blocks(array):
        return array.reshape((count, BLOCK) + array.shape[1:])
    blocks = (split_blocks(signal), split_blocks(write_key), split_blocks(read_key), split_blocks(steps), split_blocks(forgetting_exponent))
    final, outputs = lax.scan(fold, state, blocks)
    return (outputs.reshape(signal.shape), final)

def reference(tokens, w_gate, w_value, w_keys, conv_value, key_filter_taps, step, decay_rate, skip, norm_gain, w_out):
    gate = jnp.dot(tokens, w_gate, preferred_element_type=jnp.float32).astype(jnp.bfloat16)
    raw = jnp.concatenate([jnp.dot(tokens, w_value, preferred_element_type=jnp.float32), jnp.dot(tokens, w_keys, preferred_element_type=jnp.float32)], axis=1).astype(jnp.bfloat16)
    taps = jnp.concatenate([conv_value, key_filter_taps], axis=1)
    padded = jnp.concatenate([jnp.zeros((KCONV - 1, raw.shape[1]), jnp.bfloat16), raw], axis=0).astype(jnp.float32)
    summed = jnp.zeros((TOKENS, raw.shape[1]), jnp.float32)
    for tap in range(KCONV):
        summed = summed + taps[tap][None, :] * padded[tap:tap + TOKENS]
    convolved = jax.nn.silu(summed).astype(jnp.bfloat16)
    width = HEADS * P_SIZE
    signal = convolved[:, :width].astype(jnp.float32).reshape(TOKENS, HEADS, P_SIZE)
    both_keys = convolved[:, width:].astype(jnp.float32).reshape(TOKENS, GROUPS, 2, N)
    forgetting_exponent = -step * decay_rate[None, :]
    start_state = jnp.zeros((HEADS, P_SIZE, N), jnp.float32)
    output, final = ssd_blocks(signal, both_keys[:, :, 0], both_keys[:, :, 1], step, forgetting_exponent, start_state, HEADS // GROUPS)
    output = output + skip[None, :, None] * signal
    gated = output.reshape(TOKENS, width) * jax.nn.silu(gate.astype(jnp.float32))
    grouped = gated.reshape(TOKENS, GROUPS, width // GROUPS)
    reciprocal = lax.rsqrt(lax.optimization_barrier(jnp.mean(grouped * grouped, axis=-1, keepdims=True)) + 1e-05)
    normed = ((grouped * reciprocal).reshape(TOKENS, width) * norm_gain[None, :]).astype(jnp.bfloat16)
    share = width // N_TENSOR
    total = jnp.zeros((TOKENS, D), jnp.float32)
    for segment_number in range(N_TENSOR):
        term = jnp.dot(normed[:, segment_number * share:(segment_number + 1) * share], w_out[segment_number * share:(segment_number + 1) * share], preferred_element_type=jnp.float32).astype(jnp.bfloat16)
        total = total + lax.optimization_barrier(term).astype(jnp.float32)
    return total.astype(jnp.bfloat16)
```

```python
import jax
import jax.numpy as jnp
from jax import lax
from jax.experimental import pallas as pl
from jax.experimental.pallas import tpu as pltpu
from jax.sharding import Mesh, PartitionSpec as P

F32 = jnp.float32
BF16 = jnp.bfloat16
HIGHEST = lax.Precision.HIGHEST

P_SIZE = 64
N = 128
TAPS = 4
HALO = 16
BLOCK = 128
VMEM = 48 * 1024 * 1024

CONTEXT = ("z", "y")
TENSOR = ("x", "core")


def params():
    return pltpu.CompilerParams(vmem_limit_bytes=VMEM)


def one_hot_heads(heads, width):
    head = lax.broadcasted_iota(jnp.int32, (heads, width), 0)
    column = lax.broadcasted_iota(jnp.int32, (heads, width), 1)
    return (column // P_SIZE == head).astype(F32)


def dot(a, b, contract=((1,), (0,)), precision=None):
    return lax.dot_general(a, b, (contract, ((), ())), precision=precision, preferred_element_type=F32)


def silu(v):
    return v / (1.0 + jnp.exp(-v))


def decays(step, rate, spread):
    rows = step.shape[0]
    r = lax.broadcasted_iota(jnp.int32, (rows, rows), 0)
    c = lax.broadcasted_iota(jnp.int32, (rows, rows), 1)
    run = dot((r >= c).astype(F32), -step * rate, precision=HIGHEST)
    last = run[rows - 1 : rows]
    mid = 0.5 * last
    grow = dot(jnp.exp(run - mid), spread, precision=HIGHEST)
    shrink = dot(step * jnp.exp(mid - run), spread, precision=HIGHEST)
    ends = dot(
        jnp.concatenate([jnp.exp(mid), jnp.exp(last - mid), jnp.exp(last), last] * 2, axis=0),
        spread,
        precision=HIGHEST,
    )
    return grow, shrink, ends


def raw_kernel(
    order, tok, wv, wk, taps_v, taps_k, step, rate, conv_out, state_out, total_out, acc
):
    turn = pl.program_id(0)
    value = wv.shape[1]

    @pl.when(turn == 0)
    def _():
        acc[...] = jnp.zeros_like(acc)

    acc[:, :value] += dot(tok[0], wv[...])
    acc[:, value:] += dot(tok[0], wk[...])

    @pl.when(turn == pl.num_programs(0) - 1)
    def _():
        heads = step.shape[1]
        spread = one_hot_heads(heads, value)
        acc[...] = acc[...].astype(BF16).astype(F32)
        taps = jnp.concatenate([taps_v[...], taps_k[...]], axis=1)
        state = jnp.zeros((N, value), F32)
        total = jnp.zeros((1, value), F32)
        for b in range(step.shape[0] // BLOCK):
            first = b * BLOCK
            summed = jnp.zeros((BLOCK, acc.shape[1]), F32)
            for tap in range(TAPS):
                start = HALO - (TAPS - 1) + first + tap
                summed = summed + taps[tap : tap + 1] * acc[start : start + BLOCK, :]
            convolved = silu(summed).astype(BF16)
            conv_out[first : first + BLOCK, :] = convolved
            _, shrink, ends = decays(step[first : first + BLOCK, :], rate[...], spread)
            signal = (convolved[:, :value].astype(F32) * shrink).astype(BF16)
            fresh = dot(convolved[:, value : value + N], signal, ((0,), (0,)))
            state = ends[2:3] * state + ends[1:2] * fresh
            total = total + ends[3:4]
        state_out[...] = state.astype(BF16)
        total_out[...] = jnp.broadcast_to(total, total_out.shape)


def prefix_kernel(states, out):
    pieces = states.shape[0]
    rows = out.shape[1]
    state = jnp.zeros((rows, out.shape[2]), F32)
    for piece in range(pieces):
        out[piece] = state.astype(BF16)
        block = states[piece].astype(F32)
        total = block[rows : rows + 1] + block[rows + 1 : rows + 2] + block[rows + 2 : rows + 3]
        state = jnp.exp(total) * state + block[:rows]


def scan_kernel(conv, step, rate, skip, start, out):
    value = out.shape[1]
    heads = step.shape[1]
    spread = one_hot_heads(heads, value)
    direct = dot(jnp.broadcast_to(skip[...], (8, heads)), spread, precision=HIGHEST)[0:1]
    r = lax.broadcasted_iota(jnp.int32, (BLOCK, BLOCK), 0)
    c = lax.broadcasted_iota(jnp.int32, (BLOCK, BLOCK), 1)
    state = start[...].astype(F32)
    for b in range(step.shape[0] // BLOCK):
        rows = slice(b * BLOCK, (b + 1) * BLOCK)
        grow, shrink, ends = decays(step[rows, :], rate[...], spread)
        signal = conv[rows, :value].astype(F32)
        write = conv[rows, value : value + N]
        read = conv[rows, value + N :]
        scores = jnp.where(r >= c, dot(read, write, ((1,), (1,))), 0.0).astype(BF16)
        scaled = (signal * shrink).astype(BF16)
        left = jnp.concatenate([scores, read], axis=1)
        right = jnp.concatenate([scaled, (state * ends[0:1]).astype(BF16)], axis=0)
        out[rows, :] = grow * dot(left, right) + direct * signal
        state = ends[2:3] * state + ends[1:2] * dot(write, scaled, ((0,), (0,)))


def gate_kernel(order, tok, wg, output, gain, normed, acc):
    turn = pl.program_id(0)

    @pl.when(turn == 0)
    def _():
        acc[...] = jnp.zeros_like(acc)

    acc[...] += dot(tok[0, HALO:, :], wg[...])

    @pl.when(turn == pl.num_programs(0) - 1)
    def _():
        gated = output[...] * silu(acc[...].astype(BF16).astype(F32))
        mean = jnp.mean(gated * gated, axis=1, keepdims=True)
        normed[...] = (gated * lax.rsqrt(mean + 1e-05) * gain[...]).astype(BF16)


def out_kernel(normed, w, out):
    out[...] = dot(normed[...], w[...], ((1,), (1,))).astype(BF16)


def local(
    tokens,
    w_gate,
    w_value,
    w_keys,
    conv_value,
    key_filter_taps,
    step,
    decay_rate,
    skip,
    norm_gain,
    w_out,
):
    rows, depth = tokens.shape
    value, keys = w_value.shape[1], w_keys.shape[1]
    heads = step.shape[1]
    pieces = lax.axis_size(CONTEXT)
    shares = lax.axis_size(TENSOR)
    rate = decay_rate[None, :]

    weights = lax.all_gather(
        jnp.concatenate([w_value, w_gate, w_out.T, w_keys], axis=1), CONTEXT, axis=0, tiled=True
    )
    route = [(i, i + 1) for i in range(pieces - 1)]
    before = lax.ppermute(tokens[rows - HALO :], CONTEXT, route)
    whole = lax.all_gather(jnp.concatenate([before, tokens], axis=0), TENSOR)
    order = jnp.zeros((8,), jnp.int32)

    convolved, own_state, total = pl.pallas_call(
        raw_kernel,
        grid_spec=pltpu.PrefetchScalarGridSpec(
            num_scalar_prefetch=1,
            grid=(shares,),
            in_specs=[
                pl.BlockSpec((1, rows + HALO, depth), lambda k, o: (k, 0, 0)),
                pl.BlockSpec((depth, value), lambda k, o: (k, 0)),
                pl.BlockSpec((depth, keys), lambda k, o: (k, 6)),
                pl.BlockSpec(conv_value.shape, lambda k, o: (0, 0)),
                pl.BlockSpec(key_filter_taps.shape, lambda k, o: (0, 0)),
                pl.BlockSpec(step.shape, lambda k, o: (0, 0)),
                pl.BlockSpec(rate.shape, lambda k, o: (0, 0)),
            ],
            out_specs=[
                pl.BlockSpec((rows, value + keys), lambda k, o: (0, 0)),
                pl.BlockSpec((N, value), lambda k, o: (0, 0)),
                pl.BlockSpec((8, value), lambda k, o: (0, 0)),
            ],
            scratch_shapes=[pltpu.VMEM((rows + HALO, value + keys), F32)],
        ),
        out_shape=[
            jax.ShapeDtypeStruct((rows, value + keys), BF16),
            jax.ShapeDtypeStruct((N, value), BF16),
            jax.ShapeDtypeStruct((8, value), F32),
        ],
        compiler_params=params(),
        name="raw",
    )(order, whole, weights, weights, conv_value, key_filter_taps, step, rate)

    slab = N // pieces
    high = total.astype(BF16)
    rest = total - high.astype(F32)
    middle = rest.astype(BF16)
    low = (rest - middle.astype(F32)).astype(BF16)
    totals = jnp.concatenate([high[:1], middle[:1], low[:1], jnp.zeros_like(low[:1])], axis=0)
    packed = jnp.concatenate(
        [own_state.reshape(pieces, slab, value), jnp.broadcast_to(totals, (pieces, 4, value))], axis=1
    )
    slices = lax.all_to_all(packed, CONTEXT, 0, 0, tiled=True)
    starts = pl.pallas_call(
        prefix_kernel,
        out_shape=jax.ShapeDtypeStruct((pieces, slab, value), BF16),
        compiler_params=params(),
        name="prefix",
    )(slices)
    start = lax.all_to_all(starts, CONTEXT, 0, 0, tiled=True).reshape(N, value)

    output = pl.pallas_call(
        scan_kernel,
        out_shape=jax.ShapeDtypeStruct((rows, value), F32),
        compiler_params=params(),
        name="scan",
    )(convolved, step, rate, skip[None, :], start)

    normed = pl.pallas_call(
        gate_kernel,
        grid_spec=pltpu.PrefetchScalarGridSpec(
            num_scalar_prefetch=1,
            grid=(shares,),
            in_specs=[
                pl.BlockSpec((1, rows + HALO, depth), lambda k, o: (k, 0, 0)),
                pl.BlockSpec((depth, value), lambda k, o: (k, 1)),
                pl.BlockSpec((rows, value), lambda k, o: (0, 0)),
                pl.BlockSpec((1, value), lambda k, o: (0, 0)),
            ],
            out_specs=pl.BlockSpec((rows, value), lambda k, o: (0, 0)),
            scratch_shapes=[pltpu.VMEM((rows, value), F32)],
        ),
        out_shape=jax.ShapeDtypeStruct((rows, value), BF16),
        compiler_params=params(),
        name="gate",
    )(order, whole, weights, output, norm_gain[None, :])

    terms = pl.pallas_call(
        out_kernel,
        grid=(shares,),
        in_specs=[
            pl.BlockSpec((rows, value), lambda j: (0, 0)),
            pl.BlockSpec((depth, value), lambda j: (j, 2)),
        ],
        out_specs=pl.BlockSpec((rows, depth), lambda j: (0, j)),
        out_shape=jax.ShapeDtypeStruct((rows, shares * depth), BF16),
        compiler_params=params(),
        name="out",
    )(normed, weights)
    return lax.psum_scatter(terms, TENSOR, scatter_dimension=1, tiled=True)


def solution(mesh):
    fine = Mesh(mesh.devices.reshape(8, 4, 4, 2), ("z", "y", "x", "core"))
    return jax.shard_map(
        local,
        mesh=fine,
        in_specs=(
            P(CONTEXT, TENSOR),
            P(CONTEXT, TENSOR),
            P(CONTEXT, TENSOR),
            P(CONTEXT, TENSOR),
            P(None, TENSOR),
            P(None, TENSOR),
            P(CONTEXT, TENSOR),
            P(TENSOR),
            P(TENSOR),
            P(TENSOR),
            P(TENSOR, CONTEXT),
        ),
        out_specs=P(CONTEXT, TENSOR),
        check_vma=False,
    )
```

```python
import jax
import jax.numpy as jnp
from jax import lax
from jax.experimental import pallas as pl
from jax.experimental.pallas import tpu as pltpu
from jax.sharding import Mesh, PartitionSpec as P

F32 = jnp.float32
BF16 = jnp.bfloat16
HIGHEST = lax.Precision.HIGHEST

P_SIZE = 64
N = 128
TAPS = 4
HALO = 16
BLOCK = 128
CONTEXT = ("z", "y")
TENSOR = ("x", "core")


def params(mebibytes):
    return pltpu.CompilerParams(vmem_limit_bytes=mebibytes * 1024 * 1024)


def cost(flops, bytes_accessed):
    return pl.CostEstimate(flops=flops, bytes_accessed=bytes_accessed, transcendentals=0)


def one_hot_heads(heads, width):
    head = lax.broadcasted_iota(jnp.int32, (heads, width), 0)
    column = lax.broadcasted_iota(jnp.int32, (heads, width), 1)
    return (column // P_SIZE == head).astype(F32)


def dot(a, b, contract=((1,), (0,)), precision=None):
    return lax.dot_general(a, b, (contract, ((), ())), precision=precision, preferred_element_type=F32)


def silu(v):
    return v / (1.0 + jnp.exp(-v))


def decays(step, rate, spread):
    rows = step.shape[0]
    r = lax.broadcasted_iota(jnp.int32, (rows, rows), 0)
    c = lax.broadcasted_iota(jnp.int32, (rows, rows), 1)
    run = dot((r >= c).astype(F32), -step * rate, precision=HIGHEST)
    last = run[rows - 1 : rows]
    mid = 0.5 * last
    grow = dot(jnp.exp(run - mid), spread, precision=HIGHEST)
    shrink = dot(step * jnp.exp(mid - run), spread, precision=HIGHEST)
    ends = dot(
        jnp.concatenate([jnp.exp(mid), jnp.exp(last - mid), jnp.exp(last), last] * 2, axis=0),
        spread,
        precision=HIGHEST,
    )
    return grow, shrink, ends


def block_of(place, piece):
    x, core = place[2], place[3]
    other = piece // 4
    return lax.rem(x + piece % 4, 4) * 2 + (core if other == 0 else 1 - core)


def start_rows(block, y, quarters, target, sems):
    here, ahead, across, across_rest, behind = quarters
    rows = here.shape[1]

    def start(d, source, index):
        at = pl.ds(pl.multiple_of(lax.rem(y + d, 4) * rows, rows), rows)
        pltpu.make_async_copy(source.at[index], target.at[at], sems.at[d]).start()

    start(0, here, block)
    start(1, ahead, block)
    start(3, behind, block)
    half = across.shape[0]

    @pl.when(block < half)
    def _():
        start(2, across, block)

    @pl.when(block >= half)
    def _():
        start(2, across_rest, block - half)


def wait_rows(source, target, sems):
    rows = source.shape[1]
    for d in range(4):
        at = pl.ds(d * rows, rows)
        pltpu.make_async_copy(source.at[0], target.at[at], sems.at[d]).wait()


def raw_kernel(place, *refs):
    pieces, refs = refs[:8], refs[8:]
    halo, values, refs = refs[0], refs[1:6], refs[6:]
    keys, taps_v, taps_k, step, rate, *refs = refs
    conv_out, packed_out, tok, wv, wk, acc, tok_sems, halo_sems, v_sems, k_sems = refs
    rows, depth = pieces[0].shape
    value = taps_v.shape[1]
    for i in range(8):
        pltpu.make_async_copy(pieces[i], tok.at[i, pl.ds(HALO, rows)], tok_sems.at[i]).start()
        pltpu.make_async_copy(halo.at[i], tok.at[i, pl.ds(0, HALO)], halo_sems.at[i]).start()
        block = block_of(place, i)
        start_rows(block, place[1], values, wv.at[i], v_sems.at[i])
        at = pl.ds(pl.multiple_of(block * depth, depth), depth)
        pltpu.make_async_copy(keys.at[at], wk.at[i], k_sems.at[i]).start()

    acc[...] = jnp.zeros_like(acc)

    def turn(i, carry):
        pltpu.make_async_copy(pieces[0], tok.at[i, pl.ds(HALO, rows)], tok_sems.at[i]).wait()
        pltpu.make_async_copy(halo.at[i], tok.at[i, pl.ds(0, HALO)], halo_sems.at[i]).wait()
        wait_rows(values[0], wv.at[i], v_sems.at[i])
        pltpu.make_async_copy(keys.at[pl.ds(0, depth)], wk.at[i], k_sems.at[i]).wait()
        acc[:, :value] += dot(tok[i], wv[i])
        acc[:, value:] += dot(tok[i], wk[i])
        return carry

    lax.fori_loop(0, 8, turn, 0)

    heads = step.shape[1]
    spread = one_hot_heads(heads, value)
    acc[...] = acc[...].astype(BF16).astype(F32)
    taps = jnp.concatenate([taps_v[...], taps_k[...]], axis=1)
    state = jnp.zeros((N, value), F32)
    total = jnp.zeros((1, value), F32)
    for b in range(step.shape[0] // BLOCK):
        first = b * BLOCK
        summed = jnp.zeros((BLOCK, acc.shape[1]), F32)
        for tap in range(TAPS):
            start = HALO - (TAPS - 1) + first + tap
            summed = summed + taps[tap : tap + 1] * acc[start : start + BLOCK, :]
        convolved = silu(summed).astype(BF16)
        conv_out[first : first + BLOCK, :] = convolved
        _, shrink, ends = decays(step[first : first + BLOCK, :], rate[...], spread)
        signal = (convolved[:, :value].astype(F32) * shrink).astype(BF16)
        fresh = dot(convolved[:, value : value + N], signal, ((0,), (0,)))
        state = ends[2:3] * state + ends[1:2] * fresh
        total = total + ends[3:4]
    high = total.astype(BF16).astype(F32)
    middle = (total - high).astype(BF16).astype(F32)
    low = total - high - middle
    totals = jnp.concatenate([high, middle, low, jnp.zeros_like(low)], axis=0)
    for p in range(packed_out.shape[0]):
        slab = N // packed_out.shape[0]
        packed_out[p] = jnp.concatenate([state[p * slab : (p + 1) * slab], totals], axis=0).astype(BF16)


def prefix_kernel(states, earlier, out):
    pieces = states.shape[0]
    rows = out.shape[1]
    state = jnp.zeros((rows, out.shape[2]), F32)
    for piece in range(pieces):
        out[piece] = state.astype(BF16)
        block = states[piece].astype(F32)
        total = block[rows : rows + 1] + block[rows + 1 : rows + 2] + block[rows + 2 : rows + 3]
        state = jnp.exp(total) * state + block[:rows]


def scan_kernel(conv, step, rate, skip, out):
    value = out.shape[1]
    heads = step.shape[1]
    spread = one_hot_heads(heads, value)
    direct = dot(jnp.broadcast_to(skip[...], (8, heads)), spread, precision=HIGHEST)[0:1]
    r = lax.broadcasted_iota(jnp.int32, (BLOCK, BLOCK), 0)
    c = lax.broadcasted_iota(jnp.int32, (BLOCK, BLOCK), 1)
    state = jnp.zeros((N, value), F32)
    for b in range(step.shape[0] // BLOCK):
        rows = slice(b * BLOCK, (b + 1) * BLOCK)
        grow, shrink, ends = decays(step[rows, :], rate[...], spread)
        signal = conv[rows, :value].astype(F32)
        write = conv[rows, value : value + N]
        read = conv[rows, value + N :]
        scores = jnp.where(r >= c, dot(read, write, ((1,), (1,))), 0.0).astype(BF16)
        scaled = (signal * shrink).astype(BF16)
        left = jnp.concatenate([scores, read], axis=1)
        right = jnp.concatenate([scaled, (state * ends[0:1]).astype(BF16)], axis=0)
        out[rows, :] = grow * dot(left, right) + direct * signal
        state = ends[2:3] * state + ends[1:2] * dot(write, scaled, ((0,), (0,)))


def gate_kernel(place, *refs):
    pieces, refs = refs[:8], refs[8:]
    gates, refs = refs[:5], refs[5:]
    out, tok, wg, acc, tok_sems, w_sems = refs
    for i in range(8):
        pltpu.make_async_copy(pieces[i], tok.at[i], tok_sems.at[i]).start()
        start_rows(block_of(place, i), place[1], gates, wg.at[i], w_sems.at[i])

    acc[...] = jnp.zeros_like(acc)

    def turn(i, carry):
        pltpu.make_async_copy(pieces[0], tok.at[i], tok_sems.at[i]).wait()
        wait_rows(gates[0], wg.at[i], w_sems.at[i])
        acc[...] += dot(tok[i], wg[i])
        return carry

    lax.fori_loop(0, 8, turn, 0)
    out[...] = acc[...].astype(BF16)


def norm_kernel(output, conv, step, rate, start, gate, gain, normed):
    value = output.shape[1]
    spread = one_hot_heads(step.shape[1], value)
    r = lax.broadcasted_iota(jnp.int32, (BLOCK, BLOCK), 0)
    c = lax.broadcasted_iota(jnp.int32, (BLOCK, BLOCK), 1)
    lower = (r >= c).astype(F32)
    so_far = jnp.zeros((1, step.shape[1]), F32)
    before = [start[p].astype(F32) for p in range(start.shape[0])]
    before = jnp.concatenate(before, axis=0).astype(BF16)
    for b in range(step.shape[0] // BLOCK):
        rows = slice(b * BLOCK, (b + 1) * BLOCK)
        run = so_far + dot(lower, -step[rows, :] * rate[...], precision=HIGHEST)
        so_far = run[BLOCK - 1 :]
        kept = dot(jnp.exp(run), spread, precision=HIGHEST)
        total = output[rows, :] + kept * dot(conv[rows, value + N :], before)
        gated = total * silu(gate[rows, :].astype(F32))
        mean = jnp.mean(gated * gated, axis=1, keepdims=True)
        normed[rows, :] = (gated * lax.rsqrt(mean + 1e-05) * gain[...]).astype(BF16)


def out_kernel(targets, own, sibling, w_own, w_sibling, earlier, *outs):
    term = dot(own[...], w_own[...], ((1,), (1,))) + dot(sibling[...], w_sibling[...], ((1,), (1,)))
    for job, out in enumerate(outs):

        @pl.when(pl.program_id(0) == job)
        def _():
            out[...] = term.astype(out.dtype)


def shifted(array, axis, distance):
    size = lax.axis_size(axis)
    return lax.ppermute(array, axis, [((i + distance) % size, i) for i in range(size)])


def quad(array):
    near = jnp.concatenate([array] + [shifted(array, "y", d) for d in (1, 2, 3)], axis=0)
    return jnp.roll(near, lax.axis_index("y") * array.shape[0], axis=0)


def after(array, *others):
    return lax.optimization_barrier((array, *others))[0]


def local(
    tokens,
    w_gate,
    w_value,
    w_keys,
    conv_value,
    key_filter_taps,
    step,
    decay_rate,
    skip,
    norm_gain,
    w_out,
):
    rows, depth = tokens.shape
    value, keys = w_value.shape[1], w_keys.shape[1]
    heads = step.shape[1]
    pieces = lax.axis_size(CONTEXT)
    shares = lax.axis_size(TENSOR)
    rate = decay_rate[None, :]

    both = lax.all_gather(jnp.concatenate([w_value, w_gate], axis=1), "z")
    keys_four = quad(w_keys)
    swap = []
    for z in range(8):
        for c in range(2):
            swap.append((2 * z + c, 2 * z + c if z % 2 == c else 2 * (z ^ 1) + 1 - c))
    turned = lax.ppermute(after(w_out, keys_four).T, ("z", "core"), swap)
    outs_four = quad(turned)
    ahead, behind = shifted(tokens, "x", 1), shifted(tokens, "x", -1)
    across = shifted(ahead, "x", 1)
    keys_all = lax.all_gather(keys_four, "z", axis=0, tiled=True)
    both, ahead, behind, across, outs_four = after((both, ahead, behind, across, outs_four))
    v0, g0 = both[..., :value], both[..., value:]
    v1, v3 = shifted(v0, "y", 1), shifted(v0, "y", -1)
    own_all = [tokens, ahead, across, behind]
    all_tokens = own_all + [shifted(after(a, both), "core", 1) for a in own_all]
    route = [(i, i + 1) for i in range(pieces - 1)]
    halo = lax.ppermute(jnp.stack([a[rows - HALO :] for a in all_tokens]), CONTEXT, route)
    outs = lax.all_gather(outs_four, "z", axis=0, tiled=True)
    v1, v3, halo, *all_tokens = after((v1, v3, halo, *all_tokens))
    v2 = shifted(v1[:4], "y", 1), shifted(v3[4:], "y", -1)
    g0 = after(g0, *v2)
    g1, g3 = shifted(g0, "y", 1), shifted(g0, "y", -1)
    place = jnp.stack([lax.axis_index(a) for a in ("z", "y", "x", "core")]).astype(jnp.int32)

    anywhere = pl.BlockSpec(memory_space=pl.ANY)
    smem = pl.BlockSpec(memory_space=pltpu.SMEM)
    vmem = pl.BlockSpec(memory_space=pltpu.VMEM)
    convolved, packed = pl.pallas_call(
        raw_kernel,
        in_specs=[smem] + [anywhere] * 15 + [vmem] * 4,
        out_specs=[vmem] * 2,
        scratch_shapes=[
            pltpu.VMEM((8, rows + HALO, depth), BF16),
            pltpu.VMEM((8, depth, value), BF16),
            pltpu.VMEM((8, depth, keys), BF16),
            pltpu.VMEM((rows + HALO, value + keys), F32),
            pltpu.SemaphoreType.DMA((8,)),
            pltpu.SemaphoreType.DMA((8,)),
            pltpu.SemaphoreType.DMA((8, 4)),
            pltpu.SemaphoreType.DMA((8,)),
        ],
        out_shape=[
            jax.ShapeDtypeStruct((rows, value + keys), BF16),
            jax.ShapeDtypeStruct((pieces, N // pieces + 4, value), BF16),
        ],
        compiler_params=params(58),
        name="raw",
    )(
        place, *all_tokens, halo, v0, v1, *v2, v3, keys_all,
        conv_value, key_filter_taps, step, rate,
    )

    slices = lax.all_to_all(packed, CONTEXT, 0, 0, tiled=True)
    g1, g3, _ = after((g1, g3, packed))
    g2 = shifted(g1[:4], "y", 1), shifted(g3[4:], "y", -1)
    output = pl.pallas_call(
        scan_kernel,
        out_shape=jax.ShapeDtypeStruct((rows, value), F32),
        compiler_params=params(58),
        name="scan",
    )(convolved, step, rate, skip[None, :])

    starts = pl.pallas_call(
        prefix_kernel,
        in_specs=[vmem, anywhere],
        out_specs=vmem,
        out_shape=jax.ShapeDtypeStruct((pieces, N // pieces, value), BF16),
        compiler_params=params(58),
        name="prefix",
    )(slices, output)
    start = lax.all_to_all(starts, CONTEXT, 0, 0, tiled=True)

    gate = pl.pallas_call(
        gate_kernel,
        in_specs=[smem] + [anywhere] * 13,
        out_specs=vmem,
        scratch_shapes=[
            pltpu.VMEM((8, rows, depth), BF16),
            pltpu.VMEM((8, depth, value), BF16),
            pltpu.VMEM((rows, value), F32),
            pltpu.SemaphoreType.DMA((8,)),
            pltpu.SemaphoreType.DMA((8, 4)),
        ],
        out_shape=jax.ShapeDtypeStruct((rows, value), BF16),
        compiler_params=params(58),
        name="gate",
    )(place, *all_tokens, g0, g1, *g2, g3)

    normed = pl.pallas_call(
        norm_kernel,
        out_shape=jax.ShapeDtypeStruct((rows, value), BF16),
        compiler_params=params(58),
        name="norm",
    )(output, convolved, step, rate, start, gate, norm_gain[None, :])

    x, core = lax.axis_index("x"), lax.axis_index("core")

    half = rows // 2
    sibling = shifted(normed, "core", 1)

    def terms(earlier, *jobs):
        count = len(jobs)
        goals = [(x + d) % 4 * 2 + c for c in (core, 1 - core) for d, _, _ in jobs]
        goals = jnp.stack(goals + [part for _, part, _ in jobs]).astype(jnp.int32)
        part = pl.BlockSpec((half, value), lambda j, t: (t[2 * count + j], 0))
        return pl.pallas_call(
            out_kernel,
            grid_spec=pltpu.PrefetchScalarGridSpec(
                num_scalar_prefetch=1,
                grid=(count,),
                in_specs=[
                    part,
                    part,
                    pl.BlockSpec((depth, value), lambda j, t: (t[j], 0)),
                    pl.BlockSpec((depth, value), lambda j, t: (t[count + j], 0)),
                    anywhere,
                ],
                out_specs=[pl.BlockSpec((half, depth), lambda j, t: (0, 0))] * count,
            ),
            out_shape=[jax.ShapeDtypeStruct((half, depth), kind) for _, _, kind in jobs],
            compiler_params=params(58),
            cost_estimate=cost(4 * count * half * depth * value, 2 * count * depth * value),
            name="out",
        )(goals, normed, sibling, outs, outs, earlier)

    far_upper, far_lower = terms(normed, (2, 0, BF16), (2, 1, BF16))
    from_behind = shifted(far_upper, "x", -1)
    from_ahead = shifted(far_lower, "x", 1)
    lower_ahead, upper_behind, upper_ahead, lower_behind = terms(
        far_upper, (1, 1, BF16), (3, 0, BF16), (1, 0, F32), (3, 1, F32)
    )
    lower = shifted(lower_ahead, "x", -1)
    upper = shifted(upper_behind, "x", 1)
    upper_ahead = (upper_ahead + from_behind.astype(F32)).astype(BF16)
    lower_behind = (lower_behind + from_ahead.astype(F32)).astype(BF16)
    here_upper, here_lower = terms(upper_ahead, (0, 0, F32), (0, 1, F32))
    upper = here_upper + upper.astype(F32) + shifted(upper_ahead, "x", -1).astype(F32)
    lower = here_lower + lower.astype(F32) + shifted(lower_behind, "x", 1).astype(F32)
    return jnp.concatenate([upper, lower], axis=0).astype(BF16)


def solution(mesh):
    fine = Mesh(mesh.devices.reshape(8, 4, 4, 2), ("z", "y", "x", "core"))
    return jax.shard_map(
        local,
        mesh=fine,
        in_specs=(
            P(CONTEXT, TENSOR),
            P(CONTEXT, TENSOR),
            P(CONTEXT, TENSOR),
            P(CONTEXT, TENSOR),
            P(None, TENSOR),
            P(None, TENSOR),
            P(CONTEXT, TENSOR),
            P(TENSOR),
            P(TENSOR),
            P(TENSOR),
            P(TENSOR, CONTEXT),
        ),
        out_specs=P(CONTEXT, TENSOR),
        check_vma=False,
    )
```

```python
import jax
import jax.numpy as jnp
from jax import lax
from jax.experimental import pallas as pl
from jax.experimental.pallas import tpu as pltpu
from jax.sharding import Mesh, PartitionSpec as P

F32 = jnp.float32
BF16 = jnp.bfloat16

P_SIZE = 64
N = 128
TAPS = 4
HALO = 16
BLOCK = 128
CONTEXT = ("z", "y")
TENSOR = ("x", "core")


def params(mebibytes):
    return pltpu.CompilerParams(vmem_limit_bytes=mebibytes * 1024 * 1024)


def cost(flops, bytes_accessed):
    return pl.CostEstimate(flops=flops, bytes_accessed=bytes_accessed, transcendentals=0)


def parts(v, count):
    found = []
    for _ in range(count):
        found.append(v.astype(BF16).astype(F32))
        v = v - found[-1]
    return jnp.concatenate(found, axis=0).astype(BF16)


def by_column(v, width):
    heads = v.shape[0]
    head = lax.broadcasted_iota(jnp.int32, (2 * heads, width), 0) % heads
    column = lax.broadcasted_iota(jnp.int32, (2 * heads, width), 1)
    spread = (column // P_SIZE == head).astype(F32).astype(BF16)
    return dot(parts(v, 2), spread, ((0,), (0,)))


def running_sum(v):
    heads, rows = v.shape
    r = lax.broadcasted_iota(jnp.int32, (rows, rows), 0)
    c = lax.broadcasted_iota(jnp.int32, (rows, rows), 1)
    sums = dot(parts(v, 3), (r <= c).astype(F32).astype(BF16))
    return sums[:heads] + sums[heads : 2 * heads] + sums[2 * heads :]


def dot(a, b, contract=((1,), (0,))):
    return lax.dot_general(a, b, (contract, ((), ())), preferred_element_type=F32)


def silu(v):
    return 0.5 * v * (1.0 + jnp.tanh(0.5 * v))


def decays(step, rate, width):
    run = running_sum(-step * rate)
    last = run[:, run.shape[1] - 1 :]
    mid = 0.5 * last
    grow = by_column(jnp.exp(run - mid), width)
    shrink = by_column(step * jnp.exp(mid - run), width)
    ends = jnp.concatenate([jnp.exp(mid), jnp.exp(last - mid), jnp.exp(last), last] * 2, axis=1)
    return grow, shrink, by_column(ends, width)


def block_of(place, piece):
    x, core = place[2], place[3]
    other = piece // 4
    return lax.rem(x + piece % 4, 4) * 2 + (core if other == 0 else 1 - core)


def quarter_at(y, distance, rows):
    return pl.ds(pl.multiple_of(lax.rem(y + distance, 4) * rows, rows), rows)


def split_copy(block, first, rest, target, sem):
    half = first.shape[0]

    @pl.when(block < half)
    def _():
        pltpu.make_async_copy(first.at[block], target, sem).start()

    @pl.when(block >= half)
    def _():
        pltpu.make_async_copy(rest.at[block - half], target, sem).start()


def staged(start, finish):
    for i in range(3):
        start(i)
    for i in range(8):
        finish(i)
        if i + 3 < 8:
            start(i + 3)


def raw_kernel(place, *refs):
    pieces, refs = refs[:8], refs[8:]
    v0, rest0, v1, rest1, v3, rest3, out, tok, wv, tok_sems, v_sems = refs
    y = place[1]
    quarter = v0.shape[1]

    def start(i):
        pltpu.make_async_copy(pieces[i], tok.at[i], tok_sems.at[i]).start()
        for d, first, rest in ((0, v0, rest0), (1, v1, rest1), (3, v3, rest3)):
            target = wv.at[i, quarter_at(y, d, quarter)]
            split_copy(block_of(place, i), first, rest, target, v_sems.at[i, d])
        wv[i, quarter_at(y, 2, quarter), :] = jnp.zeros((quarter, wv.shape[2]), BF16)

    def finish(i):
        pltpu.make_async_copy(pieces[i], tok.at[i], tok_sems.at[i]).wait()
        for d in (0, 1, 3):
            target = wv.at[i, quarter_at(y, d, quarter)]
            pltpu.make_async_copy(v0.at[0], target, v_sems.at[i, d]).wait()
        part = dot(tok[i], wv[i])
        out[...] = part if i == 0 else out[...] + part

    staged(start, finish)


def conv_kernel(place, *refs):
    pieces, refs = refs[:8], refs[8:]
    across, across_rest, keys, value_part, taps_v, taps_k, step, rate, *refs = refs
    conv_out, packed_out, tok, wk, wv, acc, tok_sems, k_sems, v_sems = refs
    depth = tok.shape[2]
    value = taps_v.shape[1]
    y = place[1]
    quarter = across.shape[1]

    def copies(i):
        yield pltpu.make_async_copy(pieces[i], tok.at[i], tok_sems.at[i])
        at = pl.ds(pl.multiple_of(block_of(place, i) * depth, depth), depth)
        yield pltpu.make_async_copy(keys.at[at], wk.at[i], k_sems.at[i])

    def start(i):
        for copy in copies(i):
            copy.start()
        target = wv.at[pl.ds(i * quarter, quarter)]
        split_copy(block_of(place, i), across, across_rest, target, v_sems.at[i])

    def finish(i):
        for copy in copies(i):
            copy.wait()
        target = wv.at[pl.ds(i * quarter, quarter)]
        pltpu.make_async_copy(across.at[0], target, v_sems.at[i]).wait()
        key_part = dot(tok[i], wk[i])
        acc[:, value:] = key_part if i == 0 else acc[:, value:] + key_part

    staged(start, finish)
    mine = [tok[i, :, quarter_at(y, 2, quarter)] for i in range(8)]
    acc[:, :value] = value_part[...] + dot(jnp.concatenate(mine, axis=1), wv[...])
    acc[...] = acc[...].astype(BF16).astype(F32)
    taps = jnp.concatenate([taps_v[...], taps_k[...]], axis=1)
    state = jnp.zeros((N, value), F32)
    total = jnp.zeros((1, value), F32)
    for b in range(step.shape[1] // BLOCK):
        first = b * BLOCK
        summed = jnp.zeros((BLOCK, acc.shape[1]), F32)
        for tap in range(TAPS):
            start = HALO - (TAPS - 1) + first + tap
            summed = summed + taps[tap : tap + 1] * acc[start : start + BLOCK, :]
        convolved = silu(summed).astype(BF16)
        conv_out[first : first + BLOCK, :] = convolved
        _, shrink, ends = decays(step[:, first : first + BLOCK], rate[...], value)
        signal = (convolved[:, :value].astype(F32) * shrink).astype(BF16)
        fresh = dot(convolved[:, value : value + N], signal, ((0,), (0,)))
        state = ends[2:3] * state + ends[1:2] * fresh
        total = total + ends[3:4]
    high = total.astype(BF16).astype(F32)
    middle = (total - high).astype(BF16).astype(F32)
    low = total - high - middle
    totals = jnp.concatenate([high, middle, low, jnp.zeros_like(low)], axis=0)
    for p in range(packed_out.shape[0]):
        slab = N // packed_out.shape[0]
        packed_out[p] = jnp.concatenate([state[p * slab : (p + 1) * slab], totals], axis=0).astype(BF16)


def prefix_kernel(states, earlier, out):
    pieces = states.shape[0]
    rows = out.shape[1]
    state = jnp.zeros((rows, out.shape[2]), F32)
    for piece in range(pieces):
        out[piece] = state.astype(BF16)
        block = states[piece].astype(F32)
        total = block[rows : rows + 1] + block[rows + 1 : rows + 2] + block[rows + 2 : rows + 3]
        state = jnp.exp(total) * state + block[:rows]


def scan_kernel(conv, step, rate, skip, out):
    value = out.shape[1]
    direct = by_column(jnp.broadcast_to(skip[...], step.shape[:1] + (8,)), value)[0:1]
    r = lax.broadcasted_iota(jnp.int32, (BLOCK, BLOCK), 0)
    c = lax.broadcasted_iota(jnp.int32, (BLOCK, BLOCK), 1)
    state = jnp.zeros((N, value), F32)
    for b in range(step.shape[1] // BLOCK):
        rows = slice(b * BLOCK, (b + 1) * BLOCK)
        grow, shrink, ends = decays(step[:, rows], rate[...], value)
        signal = conv[rows, :value].astype(F32)
        write = conv[rows, value : value + N]
        read = conv[rows, value + N :]
        scores = jnp.where(r >= c, dot(read, write, ((1,), (1,))), 0.0).astype(BF16)
        scaled = (signal * shrink).astype(BF16)
        left = jnp.concatenate([scores, read], axis=1)
        right = jnp.concatenate([scaled, (state * ends[0:1]).astype(BF16)], axis=0)
        out[rows, :] = grow * dot(left, right) + direct * signal
        state = ends[2:3] * state + ends[1:2] * dot(write, scaled, ((0,), (0,)))


def gate_kernel(place, *refs):
    pieces, refs = refs[:8], refs[8:]
    g0, g1, across, across_rest, g3, out, tok, wg, acc, tok_sems, w_sems = refs
    y = place[1]
    quarter = g0.shape[1]

    def copies(i):
        source = pieces[i].at[pl.ds(HALO, tok.shape[1])]
        yield pltpu.make_async_copy(source, tok.at[i], tok_sems.at[i])
        for d, source in ((0, g0), (1, g1), (3, g3)):
            target = wg.at[i, quarter_at(y, d, quarter)]
            yield pltpu.make_async_copy(source.at[block_of(place, i)], target, w_sems.at[i, d])

    def start(i):
        for copy in copies(i):
            copy.start()
        target = wg.at[i, quarter_at(y, 2, quarter)]
        split_copy(block_of(place, i), across, across_rest, target, w_sems.at[i, 2])

    def finish(i):
        for copy in copies(i):
            copy.wait()
        target = wg.at[i, quarter_at(y, 2, quarter)]
        pltpu.make_async_copy(across.at[0], target, w_sems.at[i, 2]).wait()
        part = dot(tok[i], wg[i])
        acc[...] = part if i == 0 else acc[...] + part

    staged(start, finish)
    out[...] = acc[...].astype(BF16)


def norm_kernel(output, conv, step, rate, start, gate, gain, normed):
    value = output.shape[1]
    so_far = jnp.zeros((step.shape[0], 1), F32)
    before = [start[p].astype(F32) for p in range(start.shape[0])]
    before = jnp.concatenate(before, axis=0).astype(BF16)
    for b in range(step.shape[1] // BLOCK):
        rows = slice(b * BLOCK, (b + 1) * BLOCK)
        run = so_far + running_sum(-step[:, rows] * rate[...])
        so_far = run[:, BLOCK - 1 :]
        kept = by_column(jnp.exp(run), value)
        total = output[rows, :] + kept * dot(conv[rows, value + N :], before)
        gated = total * silu(gate[rows, :].astype(F32))
        mean = jnp.mean(gated * gated, axis=1, keepdims=True)
        normed[rows, :] = (gated * lax.rsqrt(mean + 1e-05) * gain[...]).astype(BF16)


def out_kernel(targets, own, sibling, w_own, w_sibling, earlier, *outs):
    half = own.shape[0] // 2
    for part in range(2):
        rows = slice(part * half, (part + 1) * half)
        term = dot(own[rows, :], w_own[0]) + dot(sibling[rows, :], w_sibling[0])
        for job in range(len(outs) // 2):

            @pl.when(pl.program_id(0) == job)
            def _():
                out = outs[2 * job + part]
                out[...] = term.astype(out.dtype)


def shifted(array, axis, distance):
    size = lax.axis_size(axis)
    return lax.ppermute(array, axis, [((i + distance) % size, i) for i in range(size)])


def quad(array, dim=0):
    near = jnp.concatenate([array] + [shifted(array, "y", d) for d in (1, 2, 3)], axis=dim)
    return jnp.roll(near, lax.axis_index("y") * array.shape[dim], axis=dim)


def after(array, *others):
    return lax.optimization_barrier((array, *others))[0]


def local(
    tokens,
    w_gate,
    w_value,
    w_keys,
    conv_value,
    key_filter_taps,
    step,
    decay_rate,
    skip,
    norm_gain,
    w_out,
):
    rows, depth = tokens.shape
    value, keys = w_value.shape[1], w_keys.shape[1]
    step = step.T
    pieces = lax.axis_size(CONTEXT)
    shares = lax.axis_size(TENSOR)
    rate = decay_rate[:, None]

    both = lax.all_gather(jnp.concatenate([w_value, w_gate], axis=1), "z")
    keys_four = quad(w_keys)
    swap = []
    for z in range(8):
        for c in range(2):
            swap.append((2 * z + c, 2 * z + c if z % 2 == c else 2 * (z ^ 1) + 1 - c))
    swapped = lax.ppermute(after(w_out, keys_four), ("z", "core"), swap)
    outs_four = quad(swapped, 1)
    route = [(i, i + 1) for i in range(pieces - 1)]
    before = lax.ppermute(tokens[rows - HALO :], CONTEXT, route)
    own = jnp.concatenate([before, tokens], axis=0)
    ahead, behind = shifted(own, "x", 1), shifted(own, "x", -1)
    split = rows // 2 + HALO
    across = jnp.concatenate(
        [shifted(ahead[:split], "x", 1), shifted(behind[split:], "x", -1)], axis=0
    )
    keys_all = lax.all_gather(keys_four, "z", axis=0, tiled=True)
    other_near = [shifted(a, "core", 1) for a in (own, ahead, behind)]
    both, ahead, behind, across, outs_four, *other_near = after(
        (both, ahead, behind, across, outs_four, *other_near)
    )
    v0 = both[:4, :, :value], both[4:, :, :value]
    g0 = both[..., value:]
    v1_first, v3_rest = shifted(v0[0], "y", 1), shifted(v0[1], "y", -1)
    v1_rest, v3_first = shifted(v0[1], "y", 1), shifted(v0[0], "y", -1)
    v2 = shifted(v1_first, "y", 1), shifted(v3_rest, "y", -1)
    other_across = shifted(across, "core", 1)
    all_tokens = [own, ahead, across, behind, *other_near[:2], other_across, other_near[2]]
    outs = lax.all_gather(outs_four, "z")
    v1, v3 = (v1_first, v1_rest), (v3_first, v3_rest)
    place = jnp.stack([lax.axis_index(a) for a in ("z", "y", "x", "core")]).astype(jnp.int32)

    anywhere = pl.BlockSpec(memory_space=pl.ANY)
    smem = pl.BlockSpec(memory_space=pltpu.SMEM)
    vmem = pl.BlockSpec(memory_space=pltpu.VMEM)
    place = jnp.stack([lax.axis_index(a) for a in ("z", "y", "x", "core")]).astype(jnp.int32)

    anywhere = pl.BlockSpec(memory_space=pl.ANY)
    smem = pl.BlockSpec(memory_space=pltpu.SMEM)
    vmem = pl.BlockSpec(memory_space=pltpu.VMEM)
    value_part = pl.pallas_call(
        raw_kernel,
        in_specs=[smem] + [anywhere] * 14,
        out_specs=vmem,
        scratch_shapes=[
            pltpu.VMEM((8, rows + HALO, depth), BF16),
            pltpu.VMEM((8, depth, value), BF16),
            pltpu.SemaphoreType.DMA((8,)),
            pltpu.SemaphoreType.DMA((8, 4)),
        ],
        out_shape=jax.ShapeDtypeStruct((rows + HALO, value), F32),
        compiler_params=params(58),
        cost_estimate=cost(2 * rows * 8 * depth * value, 12 * rows * depth * 2),
        name="raw",
    )(place, *all_tokens, *v0, *v1, *v3)
    g0 = after(g0, *v2, value_part)
    g1, g3 = shifted(g0, "y", 1), shifted(g0, "y", -1)
    convolved, packed = pl.pallas_call(
        conv_kernel,
        in_specs=[smem] + [anywhere] * 11 + [vmem] * 5,
        out_specs=[vmem] * 2,
        scratch_shapes=[
            pltpu.VMEM((8, rows + HALO, depth), BF16),
            pltpu.VMEM((8, depth, keys), BF16),
            pltpu.VMEM((8 * depth // 4, value), BF16),
            pltpu.VMEM((rows + HALO, value + keys), F32),
            pltpu.SemaphoreType.DMA((8,)),
            pltpu.SemaphoreType.DMA((8,)),
            pltpu.SemaphoreType.DMA((8,)),
        ],
        out_shape=[
            jax.ShapeDtypeStruct((rows, value + keys), BF16),
            jax.ShapeDtypeStruct((pieces, N // pieces + 4, value), BF16),
        ],
        compiler_params=params(58),
        name="conv",
    )(
        place, *all_tokens, *v2, keys_all, value_part,
        conv_value, key_filter_taps, step, rate,
    )

    slices = lax.all_to_all(packed, CONTEXT, 0, 0, tiled=True)
    g1, g3, _ = after((g1, g3, packed))
    g2 = shifted(g1[:4], "y", 1), shifted(g3[4:], "y", -1)
    output = pl.pallas_call(
        scan_kernel,
        out_shape=jax.ShapeDtypeStruct((rows, value), F32),
        compiler_params=params(58),
        name="scan",
    )(convolved, step, rate, skip[:, None])

    starts = pl.pallas_call(
        prefix_kernel,
        in_specs=[vmem, anywhere],
        out_specs=vmem,
        out_shape=jax.ShapeDtypeStruct((pieces, N // pieces, value), BF16),
        compiler_params=params(58),
        name="prefix",
    )(slices, output)
    start = lax.all_to_all(starts, CONTEXT, 0, 0, tiled=True)

    gate = pl.pallas_call(
        gate_kernel,
        in_specs=[smem] + [anywhere] * 13,
        out_specs=vmem,
        scratch_shapes=[
            pltpu.VMEM((8, rows, depth), BF16),
            pltpu.VMEM((8, depth, value), BF16),
            pltpu.VMEM((rows, value), F32),
            pltpu.SemaphoreType.DMA((8,)),
            pltpu.SemaphoreType.DMA((8, 4)),
        ],
        out_shape=jax.ShapeDtypeStruct((rows, value), BF16),
        compiler_params=params(58),
        name="gate",
    )(place, *all_tokens, g0, g1, *g2, g3)

    normed = pl.pallas_call(
        norm_kernel,
        out_shape=jax.ShapeDtypeStruct((rows, value), BF16),
        compiler_params=params(58),
        name="norm",
    )(output, convolved, step, rate, start, gate, norm_gain[None, :])

    x, core = lax.axis_index("x"), lax.axis_index("core")

    half = rows // 2
    sibling = shifted(normed, "core", 1)

    def terms(earlier, distances, *kinds):
        count = len(distances)
        goals = [(x + d) % 4 * 2 + c for c in (core, 1 - core) for d in distances]
        block = (1, depth, value)
        return pl.pallas_call(
            out_kernel,
            grid_spec=pltpu.PrefetchScalarGridSpec(
                num_scalar_prefetch=1,
                grid=(count,),
                in_specs=[
                    pl.BlockSpec((rows, value), lambda j, t: (0, 0)),
                    pl.BlockSpec((rows, value), lambda j, t: (0, 0)),
                    pl.BlockSpec(block, lambda j, t: (t[j], 0, 0)),
                    pl.BlockSpec(block, lambda j, t: (t[count + j], 0, 0)),
                    anywhere,
                ],
                out_specs=[pl.BlockSpec((half, depth), lambda j, t: (0, 0))] * (2 * count),
            ),
            out_shape=[jax.ShapeDtypeStruct((half, depth), kind) for kind in kinds],
            compiler_params=params(58),
            cost_estimate=cost(8 * count * half * depth * value, 4 * count * depth * value),
            name="out",
        )(jnp.stack(goals).astype(jnp.int32), normed, sibling, outs, outs, earlier)

    far_upper, far_lower = terms(normed, (2,), BF16, BF16)
    from_behind = shifted(far_upper, "x", -1)
    from_ahead = shifted(far_lower, "x", 1)
    upper_ahead, lower_ahead, upper_behind, lower_behind = terms(
        far_upper, (1, 3), F32, BF16, BF16, F32
    )
    lower = shifted(lower_ahead, "x", -1)
    upper = shifted(upper_behind, "x", 1)
    upper_ahead = (upper_ahead + from_behind.astype(F32)).astype(BF16)
    lower_behind = (lower_behind + from_ahead.astype(F32)).astype(BF16)
    here_upper, here_lower = terms(upper_ahead, (0,), F32, F32)
    upper = here_upper + upper.astype(F32) + shifted(upper_ahead, "x", -1).astype(F32)
    lower = here_lower + lower.astype(F32) + shifted(lower_behind, "x", 1).astype(F32)
    return jnp.concatenate([upper, lower], axis=0).astype(BF16)


def solution(mesh):
    fine = Mesh(mesh.devices.reshape(8, 4, 4, 2), ("z", "y", "x", "core"))
    return jax.shard_map(
        local,
        mesh=fine,
        in_specs=(
            P(CONTEXT, TENSOR),
            P(CONTEXT, TENSOR),
            P(CONTEXT, TENSOR),
            P(CONTEXT, TENSOR),
            P(None, TENSOR),
            P(None, TENSOR),
            P(CONTEXT, TENSOR),
            P(TENSOR),
            P(TENSOR),
            P(TENSOR),
            P(TENSOR, CONTEXT),
        ),
        out_specs=P(CONTEXT, TENSOR),
        check_vma=False,
    )
```

```python
import jax
import jax.numpy as jnp
from jax import lax
from jax.experimental import pallas as pl
from jax.experimental.pallas import tpu as pltpu
from jax.sharding import Mesh, PartitionSpec as P

F32 = jnp.float32
BF16 = jnp.bfloat16

P_SIZE = 64
N = 128
TAPS = 4
HALO = 16
BLOCK = 128
CONTEXT = ("z", "y")
TENSOR = ("x", "core")


def params(mebibytes):
    return pltpu.CompilerParams(vmem_limit_bytes=mebibytes * 1024 * 1024)


def cost(flops, bytes_accessed):
    return pl.CostEstimate(flops=flops, bytes_accessed=bytes_accessed, transcendentals=0)


def parts(v, count):
    found = []
    for _ in range(count):
        found.append(v.astype(BF16).astype(F32))
        v = v - found[-1]
    return jnp.concatenate(found, axis=0).astype(BF16)


def by_column(v, width):
    heads = v.shape[0]
    head = lax.broadcasted_iota(jnp.int32, (2 * heads, width), 0) % heads
    column = lax.broadcasted_iota(jnp.int32, (2 * heads, width), 1)
    spread = (column // P_SIZE == head).astype(F32).astype(BF16)
    return dot(parts(v, 2), spread, ((0,), (0,)))


def running_sum(v):
    heads, rows = v.shape
    r = lax.broadcasted_iota(jnp.int32, (rows, rows), 0)
    c = lax.broadcasted_iota(jnp.int32, (rows, rows), 1)
    sums = dot(parts(v, 3), (r <= c).astype(F32).astype(BF16))
    return sums[:heads] + sums[heads : 2 * heads] + sums[2 * heads :]


def dot(a, b, contract=((1,), (0,))):
    return lax.dot_general(a, b, (contract, ((), ())), preferred_element_type=F32)


def silu(v):
    return 0.5 * v * (1.0 + jnp.tanh(0.5 * v))


def decays(step, rate, width):
    run = running_sum(-step * rate)
    last = run[:, run.shape[1] - 1 :]
    mid = 0.5 * last
    grow = by_column(jnp.exp(run - mid), width)
    shrink = by_column(step * jnp.exp(mid - run), width)
    ends = jnp.concatenate([jnp.exp(mid), jnp.exp(last - mid), jnp.exp(last), last] * 2, axis=1)
    return grow, shrink, by_column(ends, width)


def block_of(place, piece):
    x, core = place[2], place[3]
    other = piece // 4
    return lax.rem(x + piece % 4, 4) * 2 + (core if other == 0 else 1 - core)


def quarter_at(y, distance, rows):
    return pl.ds(pl.multiple_of(lax.rem(y + distance, 4) * rows, rows), rows)


def split_copy(block, first, rest, target, sem):
    half = first.shape[0]

    @pl.when(block < half)
    def _():
        pltpu.make_async_copy(first.at[block], target, sem).start()

    @pl.when(block >= half)
    def _():
        pltpu.make_async_copy(rest.at[block - half], target, sem).start()


def staged(start, finish):
    for i in range(3):
        start(i)
    for i in range(8):
        finish(i)
        if i + 3 < 8:
            start(i + 3)


def raw_kernel(place, *refs):
    pieces, refs = refs[:8], refs[8:]
    v0, rest0, v1, rest1, v3, rest3, out, tok, wv, tok_sems, v_sems = refs
    y = place[1]
    quarter = v0.shape[1]

    def start(i):
        pltpu.make_async_copy(pieces[i], tok.at[i], tok_sems.at[i]).start()
        for d, first, rest in ((0, v0, rest0), (1, v1, rest1), (3, v3, rest3)):
            target = wv.at[i, quarter_at(y, d, quarter)]
            split_copy(block_of(place, i), first, rest, target, v_sems.at[i, d])
        wv[i, quarter_at(y, 2, quarter), :] = jnp.zeros((quarter, wv.shape[2]), BF16)

    def finish(i):
        pltpu.make_async_copy(pieces[i], tok.at[i], tok_sems.at[i]).wait()
        for d in (0, 1, 3):
            target = wv.at[i, quarter_at(y, d, quarter)]
            pltpu.make_async_copy(v0.at[0], target, v_sems.at[i, d]).wait()
        part = dot(tok[i], wv[i])
        out[...] = part if i == 0 else out[...] + part

    staged(start, finish)


def conv_kernel(place, *refs):
    pieces, refs = refs[:8], refs[8:]
    across, across_rest, keys, value_part, taps_v, taps_k, step, rate, *refs = refs
    conv_out, packed_out, tok, wk, wv, acc, tok_sems, k_sems, v_sems = refs
    depth = tok.shape[2]
    value = taps_v.shape[1]
    y = place[1]
    quarter = across.shape[1]

    def copies(i):
        yield pltpu.make_async_copy(pieces[i], tok.at[i], tok_sems.at[i])
        at = pl.ds(pl.multiple_of(block_of(place, i) * depth, depth), depth)
        yield pltpu.make_async_copy(keys.at[at], wk.at[i], k_sems.at[i])

    def start(i):
        for copy in copies(i):
            copy.start()
        target = wv.at[pl.ds(i * quarter, quarter)]
        split_copy(block_of(place, i), across, across_rest, target, v_sems.at[i])

    def finish(i):
        for copy in copies(i):
            copy.wait()
        target = wv.at[pl.ds(i * quarter, quarter)]
        pltpu.make_async_copy(across.at[0], target, v_sems.at[i]).wait()
        key_part = dot(tok[i], wk[i])
        acc[:, value:] = key_part if i == 0 else acc[:, value:] + key_part

    staged(start, finish)
    mine = [tok[i, :, quarter_at(y, 2, quarter)] for i in range(8)]
    acc[:, :value] = value_part[...] + dot(jnp.concatenate(mine, axis=1), wv[...])
    acc[...] = acc[...].astype(BF16).astype(F32)
    taps = jnp.concatenate([taps_v[...], taps_k[...]], axis=1)
    state = jnp.zeros((N, value), F32)
    total = jnp.zeros((1, value), F32)
    for b in range(step.shape[1] // BLOCK):
        first = b * BLOCK
        summed = jnp.zeros((BLOCK, acc.shape[1]), F32)
        for tap in range(TAPS):
            start = HALO - (TAPS - 1) + first + tap
            summed = summed + taps[tap : tap + 1] * acc[start : start + BLOCK, :]
        convolved = silu(summed).astype(BF16)
        conv_out[first : first + BLOCK, :] = convolved
        _, shrink, ends = decays(step[:, first : first + BLOCK], rate[...], value)
        signal = (convolved[:, :value].astype(F32) * shrink).astype(BF16)
        fresh = dot(convolved[:, value : value + N], signal, ((0,), (0,)))
        state = ends[2:3] * state + ends[1:2] * fresh
        total = total + ends[3:4]
    high = total.astype(BF16).astype(F32)
    middle = (total - high).astype(BF16).astype(F32)
    low = total - high - middle
    totals = jnp.concatenate([high, middle, low, jnp.zeros_like(low)], axis=0)
    for p in range(packed_out.shape[0]):
        slab = N // packed_out.shape[0]
        packed_out[p] = jnp.concatenate([state[p * slab : (p + 1) * slab], totals], axis=0).astype(BF16)


def prefix_kernel(states, earlier, out):
    pieces = states.shape[0]
    rows = out.shape[1]
    state = jnp.zeros((rows, out.shape[2]), F32)
    for piece in range(pieces):
        out[piece] = state.astype(BF16)
        block = states[piece].astype(F32)
        total = block[rows : rows + 1] + block[rows + 1 : rows + 2] + block[rows + 2 : rows + 3]
        state = jnp.exp(total) * state + block[:rows]


def scan_kernel(conv, step, rate, skip, out):
    value = out.shape[1]
    direct = by_column(jnp.broadcast_to(skip[...], step.shape[:1] + (8,)), value)[0:1]
    r = lax.broadcasted_iota(jnp.int32, (BLOCK, BLOCK), 0)
    c = lax.broadcasted_iota(jnp.int32, (BLOCK, BLOCK), 1)
    state = jnp.zeros((N, value), F32)
    for b in range(step.shape[1] // BLOCK):
        rows = slice(b * BLOCK, (b + 1) * BLOCK)
        grow, shrink, ends = decays(step[:, rows], rate[...], value)
        signal = conv[rows, :value].astype(F32)
        write = conv[rows, value : value + N]
        read = conv[rows, value + N :]
        scores = jnp.where(r >= c, dot(read, write, ((1,), (1,))), 0.0).astype(BF16)
        scaled = (signal * shrink).astype(BF16)
        left = jnp.concatenate([scores, read], axis=1)
        right = jnp.concatenate([scaled, (state * ends[0:1]).astype(BF16)], axis=0)
        out[rows, :] = grow * dot(left, right) + direct * signal
        state = ends[2:3] * state + ends[1:2] * dot(write, scaled, ((0,), (0,)))


def gate_kernel(place, *refs):
    pieces, refs = refs[:8], refs[8:]
    g0, g1, across, across_rest, g3, out, tok, wg, acc, tok_sems, w_sems = refs
    y = place[1]
    quarter = g0.shape[1]

    def copies(i):
        source = pieces[i].at[pl.ds(HALO, tok.shape[1])]
        yield pltpu.make_async_copy(source, tok.at[i], tok_sems.at[i])
        for d, source in ((0, g0), (1, g1), (3, g3)):
            target = wg.at[i, quarter_at(y, d, quarter)]
            yield pltpu.make_async_copy(source.at[block_of(place, i)], target, w_sems.at[i, d])

    def start(i):
        for copy in copies(i):
            copy.start()
        target = wg.at[i, quarter_at(y, 2, quarter)]
        split_copy(block_of(place, i), across, across_rest, target, w_sems.at[i, 2])

    def finish(i):
        for copy in copies(i):
            copy.wait()
        target = wg.at[i, quarter_at(y, 2, quarter)]
        pltpu.make_async_copy(across.at[0], target, w_sems.at[i, 2]).wait()
        part = dot(tok[i], wg[i])
        acc[...] = part if i == 0 else acc[...] + part

    staged(start, finish)
    out[...] = acc[...].astype(BF16)


def norm_kernel(output, conv, step, rate, start, gate, gain, normed):
    value = output.shape[1]
    so_far = jnp.zeros((step.shape[0], 1), F32)
    before = [start[p].astype(F32) for p in range(start.shape[0])]
    before = jnp.concatenate(before, axis=0).astype(BF16)
    for b in range(step.shape[1] // BLOCK):
        rows = slice(b * BLOCK, (b + 1) * BLOCK)
        run = so_far + running_sum(-step[:, rows] * rate[...])
        so_far = run[:, BLOCK - 1 :]
        kept = by_column(jnp.exp(run), value)
        total = output[rows, :] + kept * dot(conv[rows, value + N :], before)
        gated = total * silu(gate[rows, :].astype(F32))
        mean = jnp.mean(gated * gated, axis=1, keepdims=True)
        normed[rows, :] = (gated * lax.rsqrt(mean + 1e-05) * gain[...]).astype(BF16)


def out_kernel(targets, own, sibling, w_own, w_sibling, earlier, *outs):
    half = own.shape[0] // 2
    for part in range(2):
        rows = slice(part * half, (part + 1) * half)
        term = dot(own[rows, :], w_own[0]) + dot(sibling[rows, :], w_sibling[0])
        for job in range(len(outs) // 2):

            @pl.when(pl.program_id(0) == job)
            def _():
                out = outs[2 * job + part]
                out[...] = term.astype(out.dtype)


def shifted(array, axis, distance):
    size = lax.axis_size(axis)
    return lax.ppermute(array, axis, [((i + distance) % size, i) for i in range(size)])


def quad(array, dim=0):
    near = jnp.concatenate([array] + [shifted(array, "y", d) for d in (1, 2, 3)], axis=dim)
    return jnp.roll(near, lax.axis_index("y") * array.shape[dim], axis=dim)


def after(array, *others):
    return lax.optimization_barrier((array, *others))[0]


def local(
    tokens,
    w_gate,
    w_value,
    w_keys,
    conv_value,
    key_filter_taps,
    step,
    decay_rate,
    skip,
    norm_gain,
    w_out,
):
    rows, depth = tokens.shape
    value, keys = w_value.shape[1], w_keys.shape[1]
    step = step.T
    pieces = lax.axis_size(CONTEXT)
    shares = lax.axis_size(TENSOR)
    rate = decay_rate[:, None]

    both = lax.all_gather(jnp.concatenate([w_value, w_gate], axis=1), "z")
    keys_four = quad(w_keys)
    swap = []
    for z in range(8):
        for c in range(2):
            swap.append((2 * z + c, 2 * z + c if z % 2 == c else 2 * (z ^ 1) + 1 - c))
    swapped = lax.ppermute(after(w_out, keys_four), ("z", "core"), swap)
    outs_four = quad(swapped, 1)
    route = [(i, i + 1) for i in range(pieces - 1)]
    before = lax.ppermute(tokens[rows - HALO :], CONTEXT, route)
    own = jnp.concatenate([before, tokens], axis=0)
    ahead, behind = shifted(own, "x", 1), shifted(own, "x", -1)
    split = rows // 2 + HALO
    across = jnp.concatenate(
        [shifted(ahead[:split], "x", 1), shifted(behind[split:], "x", -1)], axis=0
    )
    keys_all = lax.all_gather(keys_four, "z", axis=0, tiled=True)
    other_near = [shifted(a, "core", 1) for a in (own, ahead, behind)]
    both, ahead, behind, across, outs_four, *other_near = after(
        (both, ahead, behind, across, outs_four, *other_near)
    )
    v0 = both[:4, :, :value], both[4:, :, :value]
    v1_first, v3_rest = shifted(v0[0], "y", 1), shifted(v0[1], "y", -1)
    v1_rest, v3_first = shifted(v0[1], "y", 1), shifted(v0[0], "y", -1)
    g0 = after(both, v1_first)[..., value:]
    v2 = shifted(v1_first, "y", 1), shifted(v3_rest, "y", -1)
    other_across = shifted(across, "core", 1)
    all_tokens = [own, ahead, across, behind, *other_near[:2], other_across, other_near[2]]
    outs = lax.all_gather(outs_four, "z")
    v1, v3 = (v1_first, v1_rest), (v3_first, v3_rest)
    place = jnp.stack([lax.axis_index(a) for a in ("z", "y", "x", "core")]).astype(jnp.int32)

    anywhere = pl.BlockSpec(memory_space=pl.ANY)
    smem = pl.BlockSpec(memory_space=pltpu.SMEM)
    vmem = pl.BlockSpec(memory_space=pltpu.VMEM)
    place = jnp.stack([lax.axis_index(a) for a in ("z", "y", "x", "core")]).astype(jnp.int32)

    anywhere = pl.BlockSpec(memory_space=pl.ANY)
    smem = pl.BlockSpec(memory_space=pltpu.SMEM)
    vmem = pl.BlockSpec(memory_space=pltpu.VMEM)
    value_part = pl.pallas_call(
        raw_kernel,
        in_specs=[smem] + [anywhere] * 14,
        out_specs=vmem,
        scratch_shapes=[
            pltpu.VMEM((8, rows + HALO, depth), BF16),
            pltpu.VMEM((8, depth, value), BF16),
            pltpu.SemaphoreType.DMA((8,)),
            pltpu.SemaphoreType.DMA((8, 4)),
        ],
        out_shape=jax.ShapeDtypeStruct((rows + HALO, value), F32),
        compiler_params=params(58),
        cost_estimate=cost(2 * rows * 8 * depth * value, 12 * rows * depth * 2),
        name="raw",
    )(place, *all_tokens, *v0, *v1, *v3)
    g0 = after(g0, *v2, value_part)
    g1, g3 = shifted(g0, "y", 1), shifted(g0, "y", -1)
    convolved, packed = pl.pallas_call(
        conv_kernel,
        in_specs=[smem] + [anywhere] * 11 + [vmem] * 5,
        out_specs=[vmem] * 2,
        scratch_shapes=[
            pltpu.VMEM((8, rows + HALO, depth), BF16),
            pltpu.VMEM((8, depth, keys), BF16),
            pltpu.VMEM((8 * depth // 4, value), BF16),
            pltpu.VMEM((rows + HALO, value + keys), F32),
            pltpu.SemaphoreType.DMA((8,)),
            pltpu.SemaphoreType.DMA((8,)),
            pltpu.SemaphoreType.DMA((8,)),
        ],
        out_shape=[
            jax.ShapeDtypeStruct((rows, value + keys), BF16),
            jax.ShapeDtypeStruct((pieces, N // pieces + 4, value), BF16),
        ],
        compiler_params=params(58),
        name="conv",
    )(
        place, *all_tokens, *v2, keys_all, value_part,
        conv_value, key_filter_taps, step, rate,
    )

    slices = lax.all_to_all(packed, CONTEXT, 0, 0, tiled=True)
    g1, g3, _ = after((g1, g3, packed))
    g2 = shifted(g1[:4], "y", 1), shifted(g3[4:], "y", -1)
    output = pl.pallas_call(
        scan_kernel,
        out_shape=jax.ShapeDtypeStruct((rows, value), F32),
        compiler_params=params(58),
        name="scan",
    )(convolved, step, rate, skip[:, None])

    starts = pl.pallas_call(
        prefix_kernel,
        in_specs=[vmem, anywhere],
        out_specs=vmem,
        out_shape=jax.ShapeDtypeStruct((pieces, N // pieces, value), BF16),
        compiler_params=params(58),
        name="prefix",
    )(slices, output)
    start = lax.all_to_all(starts, CONTEXT, 0, 0, tiled=True)

    gate = pl.pallas_call(
        gate_kernel,
        in_specs=[smem] + [anywhere] * 13,
        out_specs=vmem,
        scratch_shapes=[
            pltpu.VMEM((8, rows, depth), BF16),
            pltpu.VMEM((8, depth, value), BF16),
            pltpu.VMEM((rows, value), F32),
            pltpu.SemaphoreType.DMA((8,)),
            pltpu.SemaphoreType.DMA((8, 4)),
        ],
        out_shape=jax.ShapeDtypeStruct((rows, value), BF16),
        compiler_params=params(58),
        name="gate",
    )(place, *all_tokens, g0, g1, *g2, g3)

    normed = pl.pallas_call(
        norm_kernel,
        out_shape=jax.ShapeDtypeStruct((rows, value), BF16),
        compiler_params=params(58),
        name="norm",
    )(output, convolved, step, rate, start, gate, norm_gain[None, :])

    x, core = lax.axis_index("x"), lax.axis_index("core")

    half = rows // 2
    sibling = shifted(normed, "core", 1)

    def terms(earlier, distances, *kinds):
        count = len(distances)
        goals = [(x + d) % 4 * 2 + c for c in (core, 1 - core) for d in distances]
        block = (1, depth, value)
        return pl.pallas_call(
            out_kernel,
            grid_spec=pltpu.PrefetchScalarGridSpec(
                num_scalar_prefetch=1,
                grid=(count,),
                in_specs=[
                    pl.BlockSpec((rows, value), lambda j, t: (0, 0)),
                    pl.BlockSpec((rows, value), lambda j, t: (0, 0)),
                    pl.BlockSpec(block, lambda j, t: (t[j], 0, 0)),
                    pl.BlockSpec(block, lambda j, t: (t[count + j], 0, 0)),
                    anywhere,
                ],
                out_specs=[pl.BlockSpec((half, depth), lambda j, t: (0, 0))] * (2 * count),
            ),
            out_shape=[jax.ShapeDtypeStruct((half, depth), kind) for kind in kinds],
            compiler_params=params(58),
            cost_estimate=cost(8 * count * half * depth * value, 4 * count * depth * value),
            name="out",
        )(jnp.stack(goals).astype(jnp.int32), normed, sibling, outs, outs, earlier)

    far_upper, far_lower = terms(normed, (2,), BF16, BF16)
    from_behind = shifted(far_upper, "x", -1)
    from_ahead = shifted(far_lower, "x", 1)
    upper_ahead, lower_ahead, upper_behind, lower_behind = terms(
        far_upper, (1, 3), F32, BF16, BF16, F32
    )
    lower = shifted(lower_ahead, "x", -1)
    upper = shifted(upper_behind, "x", 1)
    upper_ahead = (upper_ahead + from_behind.astype(F32)).astype(BF16)
    lower_behind = (lower_behind + from_ahead.astype(F32)).astype(BF16)
    here_upper, here_lower = terms(upper_ahead, (0,), F32, F32)
    upper = here_upper + upper.astype(F32) + shifted(upper_ahead, "x", -1).astype(F32)
    lower = here_lower + lower.astype(F32) + shifted(lower_behind, "x", 1).astype(F32)
    return jnp.concatenate([upper, lower], axis=0).astype(BF16)


def solution(mesh):
    fine = Mesh(mesh.devices.reshape(8, 4, 4, 2), ("z", "y", "x", "core"))
    return jax.shard_map(
        local,
        mesh=fine,
        in_specs=(
            P(CONTEXT, TENSOR),
            P(CONTEXT, TENSOR),
            P(CONTEXT, TENSOR),
            P(CONTEXT, TENSOR),
            P(None, TENSOR),
            P(None, TENSOR),
            P(CONTEXT, TENSOR),
            P(TENSOR),
            P(TENSOR),
            P(TENSOR),
            P(TENSOR, CONTEXT),
        ),
        out_specs=P(CONTEXT, TENSOR),
        check_vma=False,
    )
```
